32 devices in a mesh: mp: 4 (over z), ffn: 8 (over y, x, core).
Axes of the slice: x: 2, y: 2, z: 4, core: 2. Of those that a mesh axis runs over, the one named last changes fastest.
Arguments:
- tokens: bfloat16 [1024, 8192], P('ffn', 'mp'), may hold values from -6 to 6
- gate_weight: bfloat16 [8192, 28672], P('mp', 'ffn'), may hold values from -0.0625 to 0.0625
- up_weight: bfloat16 [8192, 28672], P('mp', 'ffn'), may hold values from -0.0625 to 0.0625
- down_weight: bfloat16 [28672, 8192], P('ffn', 'mp'), may hold values from -0.03125 to 0.03125
Outputs:
- mixed: bfloat16 [1024, 8192], P('ffn', 'mp')
The draws below stay inside these ranges and needn't reach their ends.
All inputs are finite; a program needn't handle non-finite values.
Results may differ from the reference program's by a relative error of at most 0.03.
Values may be sent and summed in bfloat16 or wider, within the bound.
A program may use at most 128 MiB of HBM per device.

```python
import jax
import jax.numpy as jnp
from jax import lax

D = 8192
FF = 28672
TOKENS = 1024
N_MP = 4


def level_of(rng, dims, split, least, top_value):
    loudness, own = 1.0, jax.random.fold_in(rng, 6)
    for position, parts in split:
        steps = jnp.exp(jax.random.uniform(jax.random.fold_in(own, position), (parts,), jnp.float32, least / len(split), top_value / len(split)))
        loudness = loudness * jnp.repeat(steps, dims[position] // parts).reshape([-1 if axis == position else 1 for axis in range(len(dims))])
    return loudness


def normal_values(rng, shape, scale, bound, split=(), held_as=jnp.bfloat16):
    gain = level_of(rng, shape, split, -0.22, 0.18) if split else 1.0
    entries = jax.random.normal(rng, shape, jnp.float32) * scale * gain
    return jnp.minimum(jnp.maximum(entries, -bound), bound).astype(held_as)


def setup_inputs(seed: int = 0) -> dict:
    splits = jax.random.split(jax.random.key(seed), 5)
    tokens = normal_values(splits[0], (TOKENS, D), 1.0, 6.0, ((0, 8), (1, 4)))
    gate_weight = normal_values(splits[1], (D, FF), D ** -0.5, 0.0625, ((0, 4), (1, 8)))
    up_weight = normal_values(splits[2], (D, FF), D ** -0.5, 0.0625, ((0, 4), (1, 8)))
    down_weight = normal_values(splits[3], (FF, D), FF ** -0.5, 0.03125, ((0, 8), (1, 4)))
    return {"tokens": tokens, "gate_weight": gate_weight, "up_weight": up_weight, "down_weight": down_weight}


def reference(tokens, gate_weight, up_weight, down_weight):
    width = D // N_MP
    gate = jnp.zeros((TOKENS, FF), jnp.float32)
    up = jnp.zeros((TOKENS, FF), jnp.float32)
    for block in range(N_MP):
        lower = block * width
        block_tokens = tokens[:, lower:lower + width]
        gate_part = jnp.dot(block_tokens, gate_weight[lower:lower + width], preferred_element_type=jnp.float32).astype(jnp.bfloat16)
        up_part = jnp.dot(block_tokens, up_weight[lower:lower + width], preferred_element_type=jnp.float32).astype(jnp.bfloat16)
        gate_part, up_part = lax.optimization_barrier((gate_part, up_part))
        gate = gate + gate_part.astype(jnp.float32)
        up = up + up_part.astype(jnp.float32)
    hidden = (jax.nn.silu(gate) * up).astype(jnp.bfloat16)
    return jnp.dot(hidden, down_weight, preferred_element_type=jnp.float32).astype(jnp.bfloat16)
```

```python
import functools

import jax
import jax.numpy as jnp
from jax import lax
from jax.experimental import pallas as pl
from jax.experimental.pallas import tpu as pltpu
from jax.sharding import PartitionSpec as P

SLOTS = 12
STRIDE = 2
LAG = 0
SENDS = 3
PREFETCH = 3
MESH = pl.DeviceIdType.MESH


def widest(columns, most):
    return max(w for w in range(128, most + 1, 128) if columns % w == 0)


def xor(a, b, size):
    total, bit = 0, 1
    while bit < size:
        total = total + lax.rem(lax.div(a, bit) + lax.div(b, bit), 2) * bit
        bit *= 2
    return total


def kernel(n, peers, tokens, w_gate, w_up, w_down, out, tok, first_w, down_w,
           sum_a, sum_b, part_a, part_b, hid_a, hid_b, acc, mine, outgoing,
           load_sem, own_sem, tok_send, tok_recv, sum_send, sum_recv, credit, hid_send, hid_recv,
           out_send, out_recv, free):
    f32, bf16 = jnp.float32, jnp.bfloat16
    m, f = lax.axis_index("mp"), lax.axis_index("ffn")
    chunks, _, cols = hid_a.shape
    groups = chunks // peers
    half = groups * cols
    width = acc.shape[1]
    tile = widest(width, 512)
    tiles = width // tile
    last = n - 1
    sums, parts, hids = (sum_a, sum_b), (part_a, part_b), (hid_a, hid_b)
    depths = (m, last - m)
    ahead = (m + 1, m - 1)
    behind = (m - 1, m + 1)

    def peer_of(p):
        return xor(f, jnp.where(p == peers - 1, 1, p + 1), peers)

    def group_loads(d, j):
        columns = pl.ds(pl.multiple_of(d * half + j * cols, 128), cols)
        return (pltpu.make_async_copy(w_gate.at[:, columns], first_w.at[d * groups + j, :, pl.ds(0, cols)],
                                      load_sem.at[d, 0, j]),
                pltpu.make_async_copy(w_up.at[:, columns], first_w.at[d * groups + j, :, pl.ds(cols, cols)],
                                      load_sem.at[d, 1, j]))

    own_load = pltpu.make_async_copy(tokens, tok.at[0], own_sem.at[0])
    down_load = pltpu.make_async_copy(w_down, down_w, own_sem.at[1])
    own_load.start()

    @pl.when(depths[0] <= depths[1])
    def _():
        for load in group_loads(0, 0) + group_loads(1, 0):
            load.start()

    @pl.when(depths[0] > depths[1])
    def _():
        for load in group_loads(1, 0) + group_loads(0, 0):
            load.start()

    for j in range(1, min(PREFETCH, groups)):
        for load in group_loads(0, j) + group_loads(1, j):
            load.start()

    barrier = pltpu.get_barrier_semaphore()
    for p in range(1, peers):
        pl.semaphore_signal(barrier, inc=1, device_id={"ffn": peer_of(p)}, device_id_type=MESH)

    @pl.when(m > 0)
    def _():
        pl.semaphore_signal(barrier, inc=1, device_id={"mp": m - 1}, device_id_type=MESH)

    @pl.when(m < last)
    def _():
        pl.semaphore_signal(barrier, inc=1, device_id={"mp": m + 1}, device_id_type=MESH)

    pl.semaphore_wait(barrier, peers - 1 + jnp.where(m > 0, 1, 0) + jnp.where(m < last, 1, 0))

    def token_copy(p, peer):
        return pltpu.make_async_remote_copy(
            src_ref=tokens, dst_ref=tok.at[p],
            send_sem=tok_send.at[p], recv_sem=tok_recv.at[p],
            device_id={"ffn": peer}, device_id_type=MESH)

    def sum_copy(d, c):
        slot = lax.rem(c, SLOTS)
        return pltpu.make_async_remote_copy(
            src_ref=sums[d].at[slot], dst_ref=sums[d].at[slot],
            send_sem=sum_send.at[d, lax.rem(c, SENDS)], recv_sem=sum_recv.at[d, slot],
            device_id={"mp": ahead[d]}, device_id_type=MESH)

    def hid_copy(d, c):
        return pltpu.make_async_remote_copy(
            src_ref=hids[d].at[c], dst_ref=hids[d].at[c],
            send_sem=hid_send.at[d, lax.rem(c, SENDS)], recv_sem=hid_recv.at[d, c],
            device_id={"mp": behind[d]}, device_id_type=MESH)

    def out_copy(p, t, peer):
        columns = pl.ds(pl.multiple_of(t * tile, 128), tile)
        return pltpu.make_async_remote_copy(
            src_ref=outgoing.at[lax.rem(p, 2), :, columns], dst_ref=tok.at[p, :, columns],
            send_sem=out_send.at[lax.rem(p, 2), t], recv_sem=out_recv.at[p, t],
            device_id={"ffn": peer}, device_id_type=MESH)

    token_copy(1, peer_of(1)).start()

    def start_loads(s):
        g = s + PREFETCH

        @pl.when(g < groups)
        def _():
            for load in group_loads(0, g) + group_loads(1, g):
                load.start()

        @pl.when(g == groups)
        def _():
            down_load.start()

        q = s - groups // 2
        p = lax.div(q, groups) + 2

        @pl.when((q >= 0) & (lax.rem(q, groups) == 0) & (p < peers))
        def _():
            token_copy(p, peer_of(p)).start()

    def first_matmul(d, c):
        @pl.when((c >= 0) & (c < groups))
        def _():
            for load in group_loads(d, c):
                load.wait()

        @pl.when((c >= 0) & (c < chunks))
        def _():
            parts[d][...] = jnp.dot(
                tok[lax.div(c, groups)], first_w[d * groups + lax.rem(c, groups)],
                preferred_element_type=f32).astype(bf16)

    def first_matmuls(s):
        q = s - STRIDE * jnp.minimum(depths[0], depths[1])

        @pl.when((q >= groups) & (q < chunks) & (lax.rem(q, groups) == 0))
        def _():
            token_copy(lax.div(q, groups), f).wait_recv()

        for d in range(2):
            first_matmul(d, s - STRIDE * depths[d])

        e = s - STRIDE * jnp.maximum(depths[0], depths[1]) + 1
        p = lax.div(e, groups) - 1

        @pl.when((p >= 1) & (e <= chunks) & (lax.rem(e, groups) == 0))
        def _():
            pl.semaphore_signal(free.at[p], inc=1, device_id={"ffn": peer_of(p)}, device_id_type=MESH)

    def pass_sum(d, s):
        depth, slots, part = depths[d], sums[d], parts[d]
        c = s - STRIDE * depth

        @pl.when((c >= 0) & (c < chunks))
        def _():
            slot = lax.rem(c, SLOTS)

            @pl.when(depth > 0)
            def _():
                sum_copy(d, c).wait_recv()

            @pl.when(depth < last)
            def _():
                @pl.when(c >= SLOTS)
                def _():
                    pl.semaphore_wait(credit.at[d], 1)

                @pl.when(depth == 0)
                def _():
                    slots[slot] = part[...]

                @pl.when(depth > 0)
                def _():
                    slots[slot] = (slots[slot].astype(f32) + part[...].astype(f32)).astype(bf16)

                sum_copy(d, c).start()

            @pl.when(depth == last)
            def _():
                gate = slots[slot, :, :cols].astype(f32) + part[:, :cols].astype(f32)
                up = slots[slot, :, cols:].astype(f32) + part[:, cols:].astype(f32)
                hids[d][c] = (gate / (1.0 + jnp.exp(-gate)) * up).astype(bf16)

                @pl.when(c + SLOTS < chunks)
                def _():
                    pl.semaphore_signal(credit.at[d], inc=1, device_id={"mp": behind[d]}, device_id_type=MESH)

    def pass_hidden(d, s):
        depth = depths[d]
        c = s - STRIDE * (2 * last - depth) - LAG

        @pl.when((c >= 0) & (c < chunks))
        def _():
            @pl.when(depth < last)
            def _():
                hid_copy(d, c).wait_recv()

            @pl.when(depth > 0)
            def _():
                hid_copy(d, c).start()

    def sent(d, s):
        depth = depths[d]
        c = s - STRIDE * depth - (SENDS - 1)

        @pl.when((depth < last) & (c >= 0) & (c < chunks))
        def _():
            sum_copy(d, c).wait_send()

            @pl.when((depth > 0) & (c + SLOTS < chunks))
            def _():
                pl.semaphore_signal(credit.at[d], inc=1, device_id={"mp": behind[d]}, device_id_type=MESH)

        h = s - STRIDE * (2 * last - depth) - LAG - (SENDS - 1)

        @pl.when((depth > 0) & (h >= 0) & (h < chunks))
        def _():
            hid_copy(d, h).wait_send()

    def second_matmul(s):
        c = s - STRIDE * jnp.maximum(2 * last - m, last + m) - LAG

        @pl.when(c == 0)
        def _():
            down_load.wait()

        @pl.when((c >= 0) & (c < chunks))
        def _():
            b, j = lax.div(c, groups), lax.rem(c, groups)
            peer = peer_of(b)

            @pl.when((j == groups - 1) & (b > 0))
            def _():
                pl.semaphore_wait(free.at[b], 1)

            @pl.when(j == 0)
            def _():
                acc[...] = jnp.zeros_like(acc)

            @pl.loop(0, tiles)
            def _(t):
                columns = pl.ds(pl.multiple_of(t * tile, 128), tile)
                total = jnp.dot(hid_a[c], down_w[j, :, columns], preferred_element_type=f32)
                total += jnp.dot(hid_b[c], down_w[groups + j, :, columns], preferred_element_type=f32)
                acc[:, columns] += total

                @pl.when((j == groups - 1) & (b == 0))
                def _():
                    mine[:, columns] = acc[:, columns]

                @pl.when((j == groups - 1) & (b > 0))
                def _():
                    @pl.when(b > 2)
                    def _():
                        out_copy(b - 2, t, peer).wait_send()

                    outgoing[lax.rem(b, 2), :, columns] = acc[:, columns].astype(bf16)
                    out_copy(b, t, peer).start()

            @pl.when((j == min(2, groups - 1)) & (b > 1))
            def _():
                @pl.loop(0, tiles)
                def _(t):
                    columns = pl.ds(pl.multiple_of(t * tile, 128), tile)
                    out_copy(b - 1, t, f).wait_recv()
                    mine[:, columns] += tok[b - 1, :, columns].astype(f32)

    own_load.wait()
    first_matmuls(jnp.int32(0))

    @pl.loop(0, chunks + 2 * STRIDE * last + LAG + max(0, SENDS - 1 - STRIDE))
    def _(s):
        start_loads(s)
        pass_sum(0, s)
        pass_sum(1, s)
        sent(0, s)
        sent(1, s)
        pass_hidden(0, s)
        pass_hidden(1, s)
        first_matmuls(s + 1)
        second_matmul(s)

    for t in range(tiles):
        columns = pl.ds(t * tile, tile)
        out_copy(peers - 1, t, f).wait_recv()
        out[:, columns] = (mine[:, columns] + tok[peers - 1, :, columns].astype(f32)).astype(bf16)
    for p in range(1, peers):
        token_copy(p, f).wait_send()
    for p in range(max(1, peers - 2), peers):
        for t in range(tiles):
            out_copy(p, t, f).wait_send()


def on_device(n, peers, tokens, gate_weight, up_weight, down_weight):
    held, depth = tokens.shape
    hidden, width = down_weight.shape
    half = hidden // 2
    cols = widest(half, 256)
    groups = half // cols
    chunks = groups * peers
    bf16, f32 = jnp.bfloat16, jnp.float32
    tiles = width // widest(width, 512)
    dma, regular = pltpu.SemaphoreType.DMA, pltpu.SemaphoreType.REGULAR
    return pl.pallas_call(
        functools.partial(kernel, n, peers),
        out_shape=jax.ShapeDtypeStruct((held, width), bf16),
        in_specs=[pl.BlockSpec(memory_space=pl.ANY)] * 4,
        out_specs=pl.BlockSpec(memory_space=pltpu.VMEM),
        scratch_shapes=[
            pltpu.VMEM((peers, held, depth), bf16),
            pltpu.VMEM((2 * groups, depth, 2 * cols), bf16),
            pltpu.VMEM((2 * groups, cols, width), bf16),
            pltpu.VMEM((SLOTS, held, 2 * cols), bf16),
            pltpu.VMEM((SLOTS, held, 2 * cols), bf16),
            pltpu.VMEM((held, 2 * cols), bf16),
            pltpu.VMEM((held, 2 * cols), bf16),
            pltpu.VMEM((chunks, held, cols), bf16),
            pltpu.VMEM((chunks, held, cols), bf16),
            pltpu.VMEM((held, width), f32),
            pltpu.VMEM((held, width), f32),
            pltpu.VMEM((2, held, width), bf16),
            dma((2, 2, groups)), dma((2,)), dma((peers,)), dma((peers,)), dma((2, SENDS)), dma((2, SLOTS)),
            regular((2,)), dma((2, SENDS)), dma((2, chunks)), dma((2, tiles)), dma((peers, tiles)), regular((peers,)),
        ],
        compiler_params=pltpu.CompilerParams(
            collective_id=0, has_side_effects=True, vmem_limit_bytes=63 * 1024 * 1024),
        cost_estimate=pl.CostEstimate(
            flops=6 * peers * held * depth * hidden, bytes_accessed=6 * depth * hidden,
            transcendentals=peers * held * half),
    )(tokens, gate_weight, up_weight, down_weight.reshape(2 * groups, cols, width))


def solution(mesh):
    in_specs = (P("ffn", "mp"), P("mp", "ffn"), P("mp", "ffn"), P("ffn", "mp"))
    body = functools.partial(on_device, mesh.shape["mp"], mesh.shape["ffn"])
    return jax.shard_map(body, mesh=mesh, in_specs=in_specs, out_specs=P("ffn", "mp"), check_vma=False)
```

```python
import functools

import jax
import jax.numpy as jnp
from jax import lax
from jax.experimental import pallas as pl
from jax.experimental.pallas import tpu as pltpu
from jax.sharding import PartitionSpec as P

SLOTS = 12
STRIDE = 2
LAG = 0
SENDS = 3
PREFETCH = 2
TAIL = 2
COLS = 256
MESH = pl.DeviceIdType.MESH


def widest(columns, most):
    return max(w for w in range(128, most + 1, 128) if columns % w == 0)


def xor(a, b, size):
    total, bit = 0, 1
    while bit < size:
        total = total + lax.rem(lax.div(a, bit) + lax.div(b, bit), 2) * bit
        bit *= 2
    return total


def kernel(n, peers, tokens, w_gate, w_up, w_down, out, tok, first_w, down_w,
           sum_a, sum_b, part_a, part_b, hid_a, hid_b, acc, mine, outgoing, result,
           load_sem, own_sem, result_sem, tok_send, tok_recv, sum_send, sum_recv, credit, hid_send, hid_recv,
           out_send, out_recv, free):
    f32, bf16 = jnp.float32, jnp.bfloat16
    m, f = lax.axis_index("mp"), lax.axis_index("ffn")
    chunks, _, cols = hid_a.shape
    groups = chunks // peers
    half = groups * cols
    width = acc.shape[1]
    tile = widest(width, 512)
    tiles = width // tile
    last = n - 1
    head = groups - min(TAIL, groups - 1)
    others = (peers - 1) * groups
    sums, parts, hids = (sum_a, sum_b), (part_a, part_b), (hid_a, hid_b)
    depths = (m, last - m)
    ahead = (m + 1, m - 1)
    behind = (m - 1, m + 1)

    def peer_of(p):
        return xor(f, jnp.where(p == peers - 1, 1, p + 1), peers)

    def place(c):
        q = c - head
        own = (q < 0) | (q >= others)
        block = jnp.where(own, 0, lax.div(q, groups) + 1)
        return block, jnp.where(q < 0, c, jnp.where(own, q - others + head, lax.rem(q, groups)))

    def group_loads(d, j):
        columns = pl.ds(pl.multiple_of(d * half + j * cols, 128), cols)
        return (pltpu.make_async_copy(w_gate.at[:, columns], first_w.at[d * groups + j, :, pl.ds(0, cols)],
                                      load_sem.at[d, 0, j]),
                pltpu.make_async_copy(w_up.at[:, columns], first_w.at[d * groups + j, :, pl.ds(cols, cols)],
                                      load_sem.at[d, 1, j]))

    own_load = pltpu.make_async_copy(tokens, tok.at[0], own_sem.at[0])
    down_load = pltpu.make_async_copy(w_down, down_w, own_sem.at[1])
    own_load.start()

    @pl.when(depths[0] <= depths[1])
    def _():
        for load in group_loads(0, 0):
            load.start()

    @pl.when(depths[0] > depths[1])
    def _():
        for load in group_loads(1, 0):
            load.start()

    barrier = pltpu.get_barrier_semaphore()
    for p in range(1, peers):
        pl.semaphore_signal(barrier, inc=1, device_id={"ffn": peer_of(p)}, device_id_type=MESH)

    @pl.when(m > 0)
    def _():
        pl.semaphore_signal(barrier, inc=1, device_id={"mp": m - 1}, device_id_type=MESH)

    @pl.when(m < last)
    def _():
        pl.semaphore_signal(barrier, inc=1, device_id={"mp": m + 1}, device_id_type=MESH)

    pl.semaphore_wait(barrier, peers - 1 + jnp.where(m > 0, 1, 0) + jnp.where(m < last, 1, 0))

    def token_copy(p, peer):
        return pltpu.make_async_remote_copy(
            src_ref=tokens, dst_ref=tok.at[p],
            send_sem=tok_send.at[p], recv_sem=tok_recv.at[p],
            device_id={"ffn": peer}, device_id_type=MESH)

    def sum_copy(d, c):
        slot = lax.rem(c, SLOTS)
        return pltpu.make_async_remote_copy(
            src_ref=sums[d].at[slot], dst_ref=sums[d].at[slot],
            send_sem=sum_send.at[d, lax.rem(c, SENDS)], recv_sem=sum_recv.at[d, slot],
            device_id={"mp": ahead[d]}, device_id_type=MESH)

    def hid_copy(d, c):
        return pltpu.make_async_remote_copy(
            src_ref=hids[d].at[c], dst_ref=hids[d].at[c],
            send_sem=hid_send.at[d, lax.rem(c, SENDS)], recv_sem=hid_recv.at[d, c],
            device_id={"mp": behind[d]}, device_id_type=MESH)

    def out_copy(p, t, peer):
        columns = pl.ds(pl.multiple_of(t * tile, 128), tile)
        return pltpu.make_async_remote_copy(
            src_ref=outgoing.at[lax.rem(p, 2), :, columns], dst_ref=tok.at[p, :, columns],
            send_sem=out_send.at[lax.rem(p, 2), t], recv_sem=out_recv.at[p, t],
            device_id={"ffn": peer}, device_id_type=MESH)

    def result_copy(t):
        columns = pl.ds(pl.multiple_of(t * tile, 128), tile)
        return pltpu.make_async_copy(result.at[:, columns], out.at[:, columns], result_sem.at[t])

    token_copy(1, peer_of(1)).start()

    @pl.when(depths[0] <= depths[1])
    def _():
        for load in group_loads(1, 0):
            load.start()

    @pl.when(depths[0] > depths[1])
    def _():
        for load in group_loads(0, 0):
            load.start()

    for j in range(1, min(PREFETCH, groups)):
        for load in group_loads(0, j) + group_loads(1, j):
            load.start()

    def start_loads(s):
        g = s + PREFETCH

        @pl.when(g < groups)
        def _():
            for load in group_loads(0, g) + group_loads(1, g):
                load.start()

        @pl.when(g == groups)
        def _():
            down_load.start()

        q = s - groups // 2
        p = lax.div(q, groups) + 2

        @pl.when((q >= 0) & (lax.rem(q, groups) == 0) & (p < peers))
        def _():
            token_copy(p, peer_of(p)).start()

    def first_matmul(d, c):
        b, j = place(c)

        @pl.when(((c >= 0) & (c < head)) | ((b == 1) & (j >= head)))
        def _():
            for load in group_loads(d, j):
                load.wait()

        @pl.when((c >= 0) & (c < chunks))
        def _():
            parts[d][...] = jnp.dot(
                tok[b], first_w[d * groups + j], preferred_element_type=f32).astype(bf16)

    def first_matmuls(s):
        b, j = place(s - STRIDE * jnp.minimum(depths[0], depths[1]))

        @pl.when((b > 0) & (j == 0))
        def _():
            token_copy(b, f).wait_recv()

        for d in range(2):
            first_matmul(d, s - STRIDE * depths[d])

        p, k = place(s - STRIDE * jnp.maximum(depths[0], depths[1]))

        @pl.when((p > 0) & (k == groups - 1))
        def _():
            pl.semaphore_signal(free.at[p], inc=1, device_id={"ffn": peer_of(p)}, device_id_type=MESH)

    def pass_sum(d, s):
        depth, slots, part = depths[d], sums[d], parts[d]
        c = s - STRIDE * depth

        @pl.when((c >= 0) & (c < chunks))
        def _():
            slot = lax.rem(c, SLOTS)

            @pl.when(depth > 0)
            def _():
                sum_copy(d, c).wait_recv()

            @pl.when(depth < last)
            def _():
                @pl.when(c >= SLOTS)
                def _():
                    pl.semaphore_wait(credit.at[d], 1)

                @pl.when(depth == 0)
                def _():
                    slots[slot] = part[...]

                @pl.when(depth > 0)
                def _():
                    slots[slot] = (slots[slot].astype(f32) + part[...].astype(f32)).astype(bf16)

                sum_copy(d, c).start()

            @pl.when(depth == last)
            def _():
                gate = slots[slot, :, :cols].astype(f32) + part[:, :cols].astype(f32)
                up = slots[slot, :, cols:].astype(f32) + part[:, cols:].astype(f32)
                hids[d][c] = (gate / (1.0 + jnp.exp(-gate)) * up).astype(bf16)

                @pl.when(c + SLOTS < chunks)
                def _():
                    pl.semaphore_signal(credit.at[d], inc=1, device_id={"mp": behind[d]}, device_id_type=MESH)

    def pass_hidden(d, s):
        depth = depths[d]
        c = s - STRIDE * (2 * last - depth) - LAG

        @pl.when((c >= 0) & (c < chunks))
        def _():
            @pl.when(depth < last)
            def _():
                hid_copy(d, c).wait_recv()

            @pl.when(depth > 0)
            def _():
                hid_copy(d, c).start()

    def sent(d, s):
        depth = depths[d]
        c = s - STRIDE * depth - (SENDS - 1)

        @pl.when((depth < last) & (c >= 0) & (c < chunks))
        def _():
            sum_copy(d, c).wait_send()

            @pl.when((depth > 0) & (c + SLOTS < chunks))
            def _():
                pl.semaphore_signal(credit.at[d], inc=1, device_id={"mp": behind[d]}, device_id_type=MESH)

        h = s - STRIDE * (2 * last - depth) - LAG - (SENDS - 1)

        @pl.when((depth > 0) & (h >= 0) & (h < chunks))
        def _():
            hid_copy(d, h).wait_send()

    def second_matmul(s):
        c = s - STRIDE * jnp.maximum(2 * last - m, last + m) - LAG

        @pl.when(c == 0)
        def _():
            down_load.wait()

        @pl.when((c >= 0) & (c < chunks))
        def _():
            b, j = place(c)
            peer = peer_of(b)

            @pl.when((j == groups - 1) & (b > 0))
            def _():
                pl.semaphore_wait(free.at[b], 1)

            @pl.when((j == 0) & (b > 0))
            def _():
                acc[...] = jnp.zeros_like(acc)

            @pl.when(c == 0)
            def _():
                mine[...] = jnp.zeros_like(mine)

            @pl.loop(0, tiles)
            def _(t):
                columns = pl.ds(pl.multiple_of(t * tile, 128), tile)
                total = jnp.dot(hid_a[c], down_w[j, :, columns], preferred_element_type=f32)
                total += jnp.dot(hid_b[c], down_w[groups + j, :, columns], preferred_element_type=f32)

                @pl.when(b == 0)
                def _():
                    mine[:, columns] += total

                @pl.when(b > 0)
                def _():
                    acc[:, columns] += total

                @pl.when(c == chunks - 1)
                def _():
                    out_copy(peers - 1, t, f).wait_recv()
                    result[:, columns] = (mine[:, columns] + tok[peers - 1, :, columns].astype(f32)).astype(bf16)
                    result_copy(t).start()

                @pl.when((j == groups - 1) & (b > 0))
                def _():
                    @pl.when(b > 2)
                    def _():
                        out_copy(b - 2, t, peer).wait_send()

                    outgoing[lax.rem(b, 2), :, columns] = acc[:, columns].astype(bf16)
                    out_copy(b, t, peer).start()

            @pl.when((j == max(0, groups - 2)) & (b > 1))
            def _():
                @pl.loop(0, tiles)
                def _(t):
                    columns = pl.ds(pl.multiple_of(t * tile, 128), tile)
                    out_copy(b - 1, t, f).wait_recv()
                    mine[:, columns] += tok[b - 1, :, columns].astype(f32)

    own_load.wait()
    first_matmuls(jnp.int32(0))

    @pl.loop(0, chunks + 2 * STRIDE * last + LAG + max(0, SENDS - 1 - STRIDE))
    def _(s):
        start_loads(s)
        pass_sum(0, s)
        pass_sum(1, s)
        sent(0, s)
        sent(1, s)
        pass_hidden(0, s)
        pass_hidden(1, s)
        first_matmuls(s + 1)
        second_matmul(s)

    for p in range(1, peers):
        token_copy(p, f).wait_send()
    for p in range(max(1, peers - 2), peers):
        for t in range(tiles):
            out_copy(p, t, f).wait_send()
    for t in range(tiles):
        result_copy(t).wait()


def on_device(n, peers, tokens, gate_weight, up_weight, down_weight):
    held, depth = tokens.shape
    hidden, width = down_weight.shape
    half = hidden // 2
    cols = widest(half, COLS)
    groups = half // cols
    chunks = groups * peers
    bf16, f32 = jnp.bfloat16, jnp.float32
    tiles = width // widest(width, 512)
    dma, regular = pltpu.SemaphoreType.DMA, pltpu.SemaphoreType.REGULAR
    return pl.pallas_call(
        functools.partial(kernel, n, peers),
        out_shape=jax.ShapeDtypeStruct((held, width), bf16),
        in_specs=[pl.BlockSpec(memory_space=pl.ANY)] * 4,
        out_specs=pl.BlockSpec(memory_space=pl.ANY),
        scratch_shapes=[
            pltpu.VMEM((peers, held, depth), bf16),
            pltpu.VMEM((2 * groups, depth, 2 * cols), bf16),
            pltpu.VMEM((2 * groups, cols, width), bf16),
            pltpu.VMEM((SLOTS, held, 2 * cols), bf16),
            pltpu.VMEM((SLOTS, held, 2 * cols), bf16),
            pltpu.VMEM((held, 2 * cols), bf16),
            pltpu.VMEM((held, 2 * cols), bf16),
            pltpu.VMEM((chunks, held, cols), bf16),
            pltpu.VMEM((chunks, held, cols), bf16),
            pltpu.VMEM((held, width), f32),
            pltpu.VMEM((held, width), f32),
            pltpu.VMEM((2, held, width), bf16),
            pltpu.VMEM((held, width), bf16),
            dma((2, 2, groups)), dma((2,)), dma((tiles,)), dma((peers,)), dma((peers,)), dma((2, SENDS)), dma((2, SLOTS)),
            regular((2,)), dma((2, SENDS)), dma((2, chunks)), dma((2, tiles)), dma((peers, tiles)), regular((peers,)),
        ],
        compiler_params=pltpu.CompilerParams(
            collective_id=0, has_side_effects=True, vmem_limit_bytes=63 * 1024 * 1024),
        cost_estimate=pl.CostEstimate(
            flops=6 * peers * held * depth * hidden, bytes_accessed=6 * depth * hidden,
            transcendentals=peers * held * half),
    )(tokens, gate_weight, up_weight, down_weight.reshape(2 * groups, cols, width))


def solution(mesh):
    in_specs = (P("ffn", "mp"), P("mp", "ffn"), P("mp", "ffn"), P("ffn", "mp"))
    body = functools.partial(on_device, mesh.shape["mp"], mesh.shape["ffn"])
    return jax.shard_map(body, mesh=mesh, in_specs=in_specs, out_specs=P("ffn", "mp"), check_vma=False)
```

```python
import functools

import jax
import jax.numpy as jnp
from jax import lax
from jax.experimental import pallas as pl
from jax.experimental.pallas import tpu as pltpu
from jax.sharding import PartitionSpec as P

SLOTS = 12
SUM_STRIDE = 1
SUM_EXTRA = 1
HID_STRIDE = 2
PIECES = 2
SENDS = 4
PREFETCH = 2
TAIL = 2
COLS = 256
MESH = pl.DeviceIdType.MESH


def widest(columns, most):
    return max(w for w in range(128, most + 1, 128) if columns % w == 0)


def xor(a, b, size):
    total, bit = 0, 1
    while bit < size:
        total = total + lax.rem(lax.div(a, bit) + lax.div(b, bit), 2) * bit
        bit *= 2
    return total


def kernel(n, peers, tokens, w_gate, w_up, w_down, out, tok, first_w, down_w,
           sum_a, sum_b, part_a, part_b, hid_a, hid_b, totals, outgoing, result,
           load_sem, own_sem, result_sem, tok_send, tok_recv, sum_send, sum_recv, credit, hid_send, hid_recv,
           out_send, out_recv, free):
    f32, bf16 = jnp.float32, jnp.bfloat16
    m, f = lax.axis_index("mp"), lax.axis_index("ffn")
    chunks, _, cols = hid_a.shape
    groups = chunks // peers
    half = groups * cols
    width = totals.shape[2]
    tile = widest(width, 512)
    tiles = width // tile
    last = n - 1
    head = groups - min(TAIL, groups - 1)
    others = (peers - 1) * groups
    sums, parts, hids = (sum_a, sum_b), (part_a, part_b), (hid_a, hid_b)
    depths = (m, last - m)
    nearest, furthest = jnp.minimum(m, last - m), jnp.maximum(m, last - m)
    rows = sum_a.shape[1] // PIECES
    ahead = (m + 1, m - 1)
    behind = (m - 1, m + 1)

    def sum_step(depth):
        return SUM_STRIDE * depth + SUM_EXTRA * jnp.minimum(depth, 1)

    def hid_step(depth):
        return HID_STRIDE * (2 * last - depth)

    def peer_of(p):
        return xor(f, jnp.where(p == peers - 1, 1, p + 1), peers)

    def place(c):
        q = c - head
        own = (q < 0) | (q >= others)
        block = jnp.where(own, 0, lax.div(q, groups) + 1)
        return block, jnp.where(q < 0, c, jnp.where(own, q - others + head, lax.rem(q, groups)))

    def group_loads(d, j):
        columns = pl.ds(pl.multiple_of(d * half + j * cols, 128), cols)
        return (pltpu.make_async_copy(w_gate.at[:, columns], first_w.at[d * groups + j, :, pl.ds(0, cols)],
                                      load_sem.at[d, 0, j]),
                pltpu.make_async_copy(w_up.at[:, columns], first_w.at[d * groups + j, :, pl.ds(cols, cols)],
                                      load_sem.at[d, 1, j]))

    own_load = pltpu.make_async_copy(tokens, tok.at[0], own_sem.at[0])
    down_load = pltpu.make_async_copy(w_down, down_w, own_sem.at[1])
    own_load.start()

    @pl.when(depths[0] <= depths[1])
    def _():
        for load in group_loads(0, 0):
            load.start()

    @pl.when(depths[0] > depths[1])
    def _():
        for load in group_loads(1, 0):
            load.start()

    barrier = pltpu.get_barrier_semaphore()
    for p in range(1, peers):
        pl.semaphore_signal(barrier, inc=1, device_id={"ffn": peer_of(p)}, device_id_type=MESH)

    @pl.when(m > 0)
    def _():
        pl.semaphore_signal(barrier, inc=1, device_id={"mp": m - 1}, device_id_type=MESH)

    @pl.when(m < last)
    def _():
        pl.semaphore_signal(barrier, inc=1, device_id={"mp": m + 1}, device_id_type=MESH)

    pl.semaphore_wait(barrier, peers - 1 + jnp.where(m > 0, 1, 0) + jnp.where(m < last, 1, 0))

    def token_copy(p, peer):
        return pltpu.make_async_remote_copy(
            src_ref=tokens, dst_ref=tok.at[p],
            send_sem=tok_send.at[p], recv_sem=tok_recv.at[p],
            device_id={"ffn": peer}, device_id_type=MESH)

    def sum_copy(d, c, k):
        slot, piece = lax.rem(c, SLOTS), pl.ds(k * rows, rows)
        return pltpu.make_async_remote_copy(
            src_ref=sums[d].at[slot, piece], dst_ref=sums[d].at[slot, piece],
            send_sem=sum_send.at[d, lax.rem(c, SENDS), k], recv_sem=sum_recv.at[d, slot, k],
            device_id={"mp": ahead[d]}, device_id_type=MESH)

    def hid_copy(d, c):
        return pltpu.make_async_remote_copy(
            src_ref=hids[d].at[c], dst_ref=hids[d].at[c],
            send_sem=hid_send.at[d, lax.rem(c, SENDS)], recv_sem=hid_recv.at[d, c],
            device_id={"mp": behind[d]}, device_id_type=MESH)

    def out_copy(p, t, peer):
        columns = pl.ds(t * tile, tile)
        return pltpu.make_async_remote_copy(
            src_ref=outgoing.at[lax.rem(p, 2), :, columns], dst_ref=tok.at[p, :, columns],
            send_sem=out_send.at[lax.rem(p, 2), t], recv_sem=out_recv.at[p, t],
            device_id={"ffn": peer}, device_id_type=MESH)

    def result_copy(t):
        columns = pl.ds(t * tile, tile)
        return pltpu.make_async_copy(result.at[:, columns], out.at[:, columns], result_sem.at[t])

    token_copy(1, peer_of(1)).start()

    @pl.when(depths[0] <= depths[1])
    def _():
        for load in group_loads(1, 0):
            load.start()

    @pl.when(depths[0] > depths[1])
    def _():
        for load in group_loads(0, 0):
            load.start()

    for j in range(1, min(PREFETCH, groups)):
        for load in group_loads(0, j) + group_loads(1, j):
            load.start()

    def start_loads(s):
        g = s + PREFETCH

        @pl.when(g < groups)
        def _():
            for load in group_loads(0, g) + group_loads(1, g):
                load.start()

        @pl.when(g == groups)
        def _():
            down_load.start()

        q = s - groups // 2
        p = lax.div(q, groups) + 2

        @pl.when((q >= 0) & (lax.rem(q, groups) == 0) & (p < peers))
        def _():
            token_copy(p, peer_of(p)).start()

    def first_matmul(d, c):
        b, j = place(c)

        @pl.when(((c >= 0) & (c < head)) | ((b == 1) & (j >= head)))
        def _():
            for load in group_loads(d, j):
                load.wait()

        @pl.when((c >= 0) & (c < chunks))
        def _():
            parts[d][...] = jnp.dot(
                tok[b], first_w[d * groups + j], preferred_element_type=f32).astype(bf16)

    def first_matmuls(s):
        b, j = place(s - sum_step(nearest))

        @pl.when((b > 0) & (j == 0))
        def _():
            token_copy(b, f).wait_recv()

        for d in range(2):
            first_matmul(d, s - sum_step(depths[d]))

        p, k = place(s - sum_step(furthest))

        @pl.when((p > 0) & (k == groups - 1))
        def _():
            pl.semaphore_signal(free.at[p], inc=1, device_id={"ffn": peer_of(p)}, device_id_type=MESH)

    def pass_sum(d, k, s):
        depth, slots, part = depths[d], sums[d], parts[d]
        c = s - sum_step(depth)
        piece = pl.ds(k * rows, rows)

        @pl.when((c >= 0) & (c < chunks))
        def _():
            slot = lax.rem(c, SLOTS)

            @pl.when(depth > 0)
            def _():
                sum_copy(d, c, k).wait_recv()

            @pl.when(depth < last)
            def _():
                if k == 0:
                    @pl.when(c >= SLOTS)
                    def _():
                        pl.semaphore_wait(credit.at[d], 1)

                @pl.when(depth == 0)
                def _():
                    slots[slot, piece, :] = part[piece, :]

                @pl.when(depth > 0)
                def _():
                    total = slots[slot, piece, :].astype(f32) + part[piece, :].astype(f32)
                    slots[slot, piece, :] = total.astype(bf16)

                sum_copy(d, c, k).start()

            @pl.when(depth == last)
            def _():
                gate = slots[slot, piece, :cols].astype(f32) + part[piece, :cols].astype(f32)
                up = slots[slot, piece, cols:].astype(f32) + part[piece, cols:].astype(f32)
                hids[d][c, piece, :] = (gate / (1.0 + jnp.exp(-gate)) * up).astype(bf16)

                if k == PIECES - 1:
                    @pl.when(c + SLOTS < chunks)
                    def _():
                        pl.semaphore_signal(credit.at[d], inc=1, device_id={"mp": behind[d]}, device_id_type=MESH)

    def pass_hidden(d, s):
        depth = depths[d]
        c = s - hid_step(depth)

        @pl.when((c >= 0) & (c < chunks))
        def _():
            @pl.when(depth < last)
            def _():
                hid_copy(d, c).wait_recv()

            @pl.when(depth > 0)
            def _():
                hid_copy(d, c).start()

    def sent(d, s):
        depth = depths[d]
        c = s - sum_step(depth) - (SENDS - 1)

        @pl.when((depth < last) & (c >= 0) & (c < chunks))
        def _():
            for k in range(PIECES):
                sum_copy(d, c, k).wait_send()

            @pl.when((depth > 0) & (c + SLOTS < chunks))
            def _():
                pl.semaphore_signal(credit.at[d], inc=1, device_id={"mp": behind[d]}, device_id_type=MESH)

        h = s - hid_step(depth) - (SENDS - 1)

        @pl.when((depth > 0) & (h >= 0) & (h < chunks))
        def _():
            hid_copy(d, h).wait_send()

    def second_matmul(s):
        c = s - hid_step(nearest)

        @pl.when(c == 0)
        def _():
            down_load.wait()

        @pl.when((c >= 0) & (c < chunks))
        def _():
            b, j = place(c)
            peer = peer_of(b)

            to = jnp.minimum(b, 1)

            @pl.when(j == 0)
            def _():
                totals[to] = jnp.zeros(totals.shape[1:], f32)

            product = jnp.dot(hid_a[c], down_w[j], preferred_element_type=f32)
            product += jnp.dot(hid_b[c], down_w[groups + j], preferred_element_type=f32)
            totals[to] += product

            @pl.when(c == chunks - 1)
            def _():
                for t in range(tiles):
                    columns = pl.ds(t * tile, tile)
                    out_copy(peers - 1, t, f).wait_recv()
                    total = totals[0, :, columns] + tok[peers - 1, :, columns].astype(f32)
                    result[:, columns] = total.astype(bf16)
                    result_copy(t).start()

            @pl.when((j == groups - 1) & (b > 0))
            def _():
                pl.semaphore_wait(free.at[b], 1)
                for t in range(tiles):
                    @pl.when(b > 2)
                    def _():
                        out_copy(b - 2, t, peer).wait_send()

                    columns = pl.ds(t * tile, tile)
                    outgoing[lax.rem(b, 2), :, columns] = totals[1, :, columns].astype(bf16)
                    out_copy(b, t, peer).start()

            @pl.when((j == max(0, groups - 2)) & (b > 1))
            def _():
                for t in range(tiles):
                    columns = pl.ds(t * tile, tile)
                    out_copy(b - 1, t, f).wait_recv()
                    totals[0, :, columns] += tok[b - 1, :, columns].astype(f32)

    own_load.wait()
    first_matmuls(jnp.int32(0))

    @pl.loop(0, chunks + 2 * HID_STRIDE * last + max(0, SENDS - 1 - HID_STRIDE))
    def _(s):
        for k in range(PIECES):
            pass_sum(0, k, s)
            pass_sum(1, k, s)
        pass_hidden(0, s)
        pass_hidden(1, s)
        start_loads(s)
        first_matmuls(s + 1)
        sent(0, s)
        sent(1, s)
        second_matmul(s)

    for p in range(1, peers):
        token_copy(p, f).wait_send()
    for p in range(max(1, peers - 2), peers):
        for t in range(tiles):
            out_copy(p, t, f).wait_send()
    for t in range(tiles):
        result_copy(t).wait()


def on_device(n, peers, tokens, gate_weight, up_weight, down_weight):
    held, depth = tokens.shape
    hidden, width = down_weight.shape
    half = hidden // 2
    cols = widest(half, COLS)
    groups = half // cols
    chunks = groups * peers
    bf16, f32 = jnp.bfloat16, jnp.float32
    tiles = width // widest(width, 512)
    dma, regular = pltpu.SemaphoreType.DMA, pltpu.SemaphoreType.REGULAR
    return pl.pallas_call(
        functools.partial(kernel, n, peers),
        out_shape=jax.ShapeDtypeStruct((held, width), bf16),
        in_specs=[pl.BlockSpec(memory_space=pl.ANY)] * 4,
        out_specs=pl.BlockSpec(memory_space=pl.ANY),
        scratch_shapes=[
            pltpu.VMEM((peers, held, depth), bf16),
            pltpu.VMEM((2 * groups, depth, 2 * cols), bf16),
            pltpu.VMEM((2 * groups, cols, width), bf16),
            pltpu.VMEM((SLOTS, held, 2 * cols), bf16),
            pltpu.VMEM((SLOTS, held, 2 * cols), bf16),
            pltpu.VMEM((held, 2 * cols), bf16),
            pltpu.VMEM((held, 2 * cols), bf16),
            pltpu.VMEM((chunks, held, cols), bf16),
            pltpu.VMEM((chunks, held, cols), bf16),
            pltpu.VMEM((2, held, width), f32),
            pltpu.VMEM((2, held, width), bf16),
            pltpu.VMEM((held, width), bf16),
            dma((2, 2, groups)), dma((2,)), dma((tiles,)), dma((peers,)), dma((peers,)), dma((2, SENDS, PIECES)), dma((2, SLOTS, PIECES)),
            regular((2,)), dma((2, SENDS)), dma((2, chunks)), dma((2, tiles)), dma((peers, tiles)), regular((peers,)),
        ],
        compiler_params=pltpu.CompilerParams(
            collective_id=0, has_side_effects=True, vmem_limit_bytes=63 * 1024 * 1024),
        cost_estimate=pl.CostEstimate(
            flops=6 * peers * held * depth * hidden, bytes_accessed=6 * depth * hidden,
            transcendentals=peers * held * half),
    )(tokens, gate_weight, up_weight, down_weight.reshape(2 * groups, cols, width))


def solution(mesh):
    in_specs = (P("ffn", "mp"), P("mp", "ffn"), P("mp", "ffn"), P("ffn", "mp"))
    body = functools.partial(on_device, mesh.shape["mp"], mesh.shape["ffn"])
    return jax.shard_map(body, mesh=mesh, in_specs=in_specs, out_specs=P("ffn", "mp"), check_vma=False)
```

```python
import functools

import jax
import jax.numpy as jnp
from jax import lax
from jax.experimental import pallas as pl
from jax.experimental.pallas import tpu as pltpu
from jax.sharding import PartitionSpec as P

SLOTS = 12
SUM_STRIDE = 1
SUM_EXTRA = 1
HID_STRIDE = 2
PIECES = 4
SENDS = 4
PREFETCH = 2
TAIL = 2
COLS = 256
MESH = pl.DeviceIdType.MESH


def widest(columns, most):
    return max(w for w in range(128, most + 1, 128) if columns % w == 0)


def xor(a, b, size):
    total, bit = 0, 1
    while bit < size:
        total = total + lax.rem(lax.div(a, bit) + lax.div(b, bit), 2) * bit
        bit *= 2
    return total


def kernel(n, peers, tokens, w_gate, w_up, w_down, out, tok, first_w, down_w,
           sum_a, sum_b, part_a, part_b, hid_a, hid_b, totals, outgoing, result,
           load_sem, own_sem, result_sem, tok_send, tok_recv, sum_send, sum_recv, credit, hid_send, hid_recv,
           out_send, out_recv, free):
    f32, bf16 = jnp.float32, jnp.bfloat16
    m, f = lax.axis_index("mp"), lax.axis_index("ffn")
    chunks, _, cols = hid_a.shape
    groups = chunks // peers
    half = groups * cols
    width = totals.shape[2]
    tile = widest(width, 512)
    tiles = width // tile
    last = n - 1
    head = groups - min(TAIL, groups - 1)
    others = (peers - 1) * groups
    sums, parts, hids = (sum_a, sum_b), (part_a, part_b), (hid_a, hid_b)
    depths = (m, last - m)
    nearest, furthest = jnp.minimum(m, last - m), jnp.maximum(m, last - m)
    rows = sum_a.shape[1] // PIECES
    ahead = (m + 1, m - 1)
    behind = (m - 1, m + 1)

    def sum_step(depth):
        return SUM_STRIDE * depth + SUM_EXTRA * jnp.minimum(depth, 1)

    def hid_step(depth):
        return HID_STRIDE * (2 * last - depth)

    def peer_of(p):
        return xor(f, jnp.where(p == peers - 1, 1, p + 1), peers)

    def place(c):
        q = c - head
        own = (q < 0) | (q >= others)
        block = jnp.where(own, 0, lax.div(q, groups) + 1)
        return block, jnp.where(q < 0, c, jnp.where(own, q - others + head, lax.rem(q, groups)))

    def group_loads(d, j):
        columns = pl.ds(pl.multiple_of(d * half + j * cols, 128), cols)
        return (pltpu.make_async_copy(w_gate.at[:, columns], first_w.at[d * groups + j, :, pl.ds(0, cols)],
                                      load_sem.at[d, 0, j]),
                pltpu.make_async_copy(w_up.at[:, columns], first_w.at[d * groups + j, :, pl.ds(cols, cols)],
                                      load_sem.at[d, 1, j]))

    own_load = pltpu.make_async_copy(tokens, tok.at[0], own_sem.at[0])
    down_load = pltpu.make_async_copy(w_down, down_w, own_sem.at[1])
    own_load.start()

    @pl.when(depths[0] <= depths[1])
    def _():
        for load in group_loads(0, 0):
            load.start()

    @pl.when(depths[0] > depths[1])
    def _():
        for load in group_loads(1, 0):
            load.start()

    barrier = pltpu.get_barrier_semaphore()
    for p in range(1, peers):
        pl.semaphore_signal(barrier, inc=1, device_id={"ffn": peer_of(p)}, device_id_type=MESH)

    @pl.when(m > 0)
    def _():
        pl.semaphore_signal(barrier, inc=1, device_id={"mp": m - 1}, device_id_type=MESH)

    @pl.when(m < last)
    def _():
        pl.semaphore_signal(barrier, inc=1, device_id={"mp": m + 1}, device_id_type=MESH)

    pl.semaphore_wait(barrier, peers - 1 + jnp.where(m > 0, 1, 0) + jnp.where(m < last, 1, 0))

    def token_copy(p, peer):
        return pltpu.make_async_remote_copy(
            src_ref=tokens, dst_ref=tok.at[p],
            send_sem=tok_send.at[p], recv_sem=tok_recv.at[p],
            device_id={"ffn": peer}, device_id_type=MESH)

    def sum_copy(d, c, k):
        slot, piece = lax.rem(c, SLOTS), pl.ds(k * rows, rows)
        return pltpu.make_async_remote_copy(
            src_ref=sums[d].at[slot, piece], dst_ref=sums[d].at[slot, piece],
            send_sem=sum_send.at[d, lax.rem(c, SENDS), k], recv_sem=sum_recv.at[d, slot, k],
            device_id={"mp": ahead[d]}, device_id_type=MESH)

    def hid_copy(d, c):
        return pltpu.make_async_remote_copy(
            src_ref=hids[d].at[c], dst_ref=hids[d].at[c],
            send_sem=hid_send.at[d, lax.rem(c, SENDS)], recv_sem=hid_recv.at[d, c],
            device_id={"mp": behind[d]}, device_id_type=MESH)

    def out_copy(p, t, peer):
        columns = pl.ds(t * tile, tile)
        return pltpu.make_async_remote_copy(
            src_ref=outgoing.at[lax.rem(p, 2), :, columns], dst_ref=tok.at[p, :, columns],
            send_sem=out_send.at[lax.rem(p, 2), t], recv_sem=out_recv.at[p, t],
            device_id={"ffn": peer}, device_id_type=MESH)

    def result_copy(t):
        columns = pl.ds(t * tile, tile)
        return pltpu.make_async_copy(result.at[:, columns], out.at[:, columns], result_sem.at[t])

    token_copy(1, peer_of(1)).start()

    @pl.when(depths[0] <= depths[1])
    def _():
        for load in group_loads(1, 0):
            load.start()

    @pl.when(depths[0] > depths[1])
    def _():
        for load in group_loads(0, 0):
            load.start()

    for j in range(1, min(PREFETCH, groups)):
        for load in group_loads(0, j) + group_loads(1, j):
            load.start()

    def start_loads(s):
        g = s + PREFETCH

        @pl.when(g < groups)
        def _():
            for load in group_loads(0, g) + group_loads(1, g):
                load.start()

        @pl.when(g == groups)
        def _():
            down_load.start()

        q = s - groups // 2
        p = lax.div(q, groups) + 2

        @pl.when((q >= 0) & (lax.rem(q, groups) == 0) & (p < peers))
        def _():
            token_copy(p, peer_of(p)).start()

    def first_matmul(d, c):
        b, j = place(c)

        @pl.when(((c >= 0) & (c < head)) | ((b == 1) & (j >= head)))
        def _():
            for load in group_loads(d, j):
                load.wait()

        @pl.when((c >= 0) & (c < chunks))
        def _():
            parts[d][...] = jnp.dot(
                tok[b], first_w[d * groups + j], preferred_element_type=f32).astype(bf16)

    def first_matmuls(s):
        b, j = place(s - sum_step(nearest))

        @pl.when((b > 0) & (j == 0))
        def _():
            token_copy(b, f).wait_recv()

        for d in range(2):
            first_matmul(d, s - sum_step(depths[d]))

        p, k = place(s - sum_step(furthest))

        @pl.when((p > 0) & (k == groups - 1))
        def _():
            pl.semaphore_signal(free.at[p], inc=1, device_id={"ffn": peer_of(p)}, device_id_type=MESH)

    def pass_sum(d, k, s):
        depth, slots, part = depths[d], sums[d], parts[d]
        c = s - sum_step(depth)
        piece = pl.ds(k * rows, rows)

        @pl.when((c >= 0) & (c < chunks))
        def _():
            slot = lax.rem(c, SLOTS)

            @pl.when(depth > 0)
            def _():
                sum_copy(d, c, k).wait_recv()

            @pl.when(depth < last)
            def _():
                if k == 0:
                    @pl.when(c >= SLOTS)
                    def _():
                        pl.semaphore_wait(credit.at[d], 1)

                @pl.when(depth == 0)
                def _():
                    slots[slot, piece, :] = part[piece, :]

                @pl.when(depth > 0)
                def _():
                    total = slots[slot, piece, :].astype(f32) + part[piece, :].astype(f32)
                    slots[slot, piece, :] = total.astype(bf16)

                sum_copy(d, c, k).start()

            @pl.when(depth == last)
            def _():
                gate = slots[slot, piece, :cols].astype(f32) + part[piece, :cols].astype(f32)
                up = slots[slot, piece, cols:].astype(f32) + part[piece, cols:].astype(f32)
                hids[d][c, piece, :] = (gate / (1.0 + jnp.exp(-gate)) * up).astype(bf16)

                if k == PIECES - 1:
                    @pl.when(c + SLOTS < chunks)
                    def _():
                        pl.semaphore_signal(credit.at[d], inc=1, device_id={"mp": behind[d]}, device_id_type=MESH)

    def pass_hidden(d, s):
        depth = depths[d]
        c = s - hid_step(depth)

        @pl.when((c >= 0) & (c < chunks))
        def _():
            @pl.when(depth < last)
            def _():
                hid_copy(d, c).wait_recv()

            @pl.when(depth > 0)
            def _():
                hid_copy(d, c).start()

    def sent(d, s):
        depth = depths[d]
        c = s - sum_step(depth) - (SENDS - 1)

        @pl.when((depth < last) & (c >= 0) & (c < chunks))
        def _():
            for k in range(PIECES):
                sum_copy(d, c, k).wait_send()

            @pl.when((depth > 0) & (c + SLOTS < chunks))
            def _():
                pl.semaphore_signal(credit.at[d], inc=1, device_id={"mp": behind[d]}, device_id_type=MESH)

        h = s - hid_step(depth) - (SENDS - 1)

        @pl.when((depth > 0) & (h >= 0) & (h < chunks))
        def _():
            hid_copy(d, h).wait_send()

    def second_matmul(s):
        c = s - hid_step(nearest)

        @pl.when(c == 0)
        def _():
            down_load.wait()

        @pl.when((c >= 0) & (c < chunks))
        def _():
            b, j = place(c)
            peer = peer_of(b)

            to = jnp.minimum(b, 1)

            @pl.when(j == 0)
            def _():
                totals[to] = jnp.zeros(totals.shape[1:], f32)

            product = jnp.dot(hid_a[c], down_w[j], preferred_element_type=f32)
            product += jnp.dot(hid_b[c], down_w[groups + j], preferred_element_type=f32)
            totals[to] += product

            @pl.when(c == chunks - 1)
            def _():
                for t in range(tiles):
                    columns = pl.ds(t * tile, tile)
                    out_copy(peers - 1, t, f).wait_recv()
                    total = totals[0, :, columns] + tok[peers - 1, :, columns].astype(f32)
                    result[:, columns] = total.astype(bf16)
                    result_copy(t).start()

            @pl.when((j == groups - 1) & (b > 0))
            def _():
                pl.semaphore_wait(free.at[b], 1)
                for t in range(tiles):
                    @pl.when(b > 2)
                    def _():
                        out_copy(b - 2, t, peer).wait_send()

                    columns = pl.ds(t * tile, tile)
                    outgoing[lax.rem(b, 2), :, columns] = totals[1, :, columns].astype(bf16)
                    out_copy(b, t, peer).start()

            @pl.when((j == max(0, groups - 2)) & (b > 1))
            def _():
                for t in range(tiles):
                    columns = pl.ds(t * tile, tile)
                    out_copy(b - 1, t, f).wait_recv()
                    totals[0, :, columns] += tok[b - 1, :, columns].astype(f32)

    own_load.wait()
    first_matmuls(jnp.int32(0))

    @pl.loop(0, chunks + 2 * HID_STRIDE * last + max(0, SENDS - 1 - HID_STRIDE))
    def _(s):
        for k in range(PIECES):
            pass_sum(0, k, s)
            pass_sum(1, k, s)
        pass_hidden(0, s)
        pass_hidden(1, s)
        start_loads(s)
        first_matmuls(s + 1)
        sent(0, s)
        sent(1, s)
        second_matmul(s)

    for p in range(1, peers):
        token_copy(p, f).wait_send()
    for p in range(max(1, peers - 2), peers):
        for t in range(tiles):
            out_copy(p, t, f).wait_send()
    for t in range(tiles):
        result_copy(t).wait()


def on_device(n, peers, tokens, gate_weight, up_weight, down_weight):
    held, depth = tokens.shape
    hidden, width = down_weight.shape
    half = hidden // 2
    cols = widest(half, COLS)
    groups = half // cols
    chunks = groups * peers
    bf16, f32 = jnp.bfloat16, jnp.float32
    tiles = width // widest(width, 512)
    dma, regular = pltpu.SemaphoreType.DMA, pltpu.SemaphoreType.REGULAR
    return pl.pallas_call(
        functools.partial(kernel, n, peers),
        out_shape=jax.ShapeDtypeStruct((held, width), bf16),
        in_specs=[pl.BlockSpec(memory_space=pl.ANY)] * 4,
        out_specs=pl.BlockSpec(memory_space=pl.ANY),
        scratch_shapes=[
            pltpu.VMEM((peers, held, depth), bf16),
            pltpu.VMEM((2 * groups, depth, 2 * cols), bf16),
            pltpu.VMEM((2 * groups, cols, width), bf16),
            pltpu.VMEM((SLOTS, held, 2 * cols), bf16),
            pltpu.VMEM((SLOTS, held, 2 * cols), bf16),
            pltpu.VMEM((held, 2 * cols), bf16),
            pltpu.VMEM((held, 2 * cols), bf16),
            pltpu.VMEM((chunks, held, cols), bf16),
            pltpu.VMEM((chunks, held, cols), bf16),
            pltpu.VMEM((2, held, width), f32),
            pltpu.VMEM((2, held, width), bf16),
            pltpu.VMEM((held, width), bf16),
            dma((2, 2, groups)), dma((2,)), dma((tiles,)), dma((peers,)), dma((peers,)), dma((2, SENDS, PIECES)), dma((2, SLOTS, PIECES)),
            regular((2,)), dma((2, SENDS)), dma((2, chunks)), dma((2, tiles)), dma((peers, tiles)), regular((peers,)),
        ],
        compiler_params=pltpu.CompilerParams(
            collective_id=0, has_side_effects=True, vmem_limit_bytes=63 * 1024 * 1024),
        cost_estimate=pl.CostEstimate(
            flops=6 * peers * held * depth * hidden, bytes_accessed=6 * depth * hidden,
            transcendentals=peers * held * half),
    )(tokens, gate_weight, up_weight, down_weight.reshape(2 * groups, cols, width))


def solution(mesh):
    in_specs = (P("ffn", "mp"), P("mp", "ffn"), P("mp", "ffn"), P("ffn", "mp"))
    body = functools.partial(on_device, mesh.shape["mp"], mesh.shape["ffn"])
    return jax.shard_map(body, mesh=mesh, in_specs=in_specs, out_specs=P("ffn", "mp"), check_vma=False)
```
